768 devices in a mesh: blk: 192 (over y, z, core), mpo: 4 (over x).
Axes of the slice: x: 4, y: 8, z: 12, core: 2. Of those that a mesh axis runs over, the one named last changes fastest.
Arguments:
- psi: bfloat16 [768, 256, 256], P('blk'), may hold values from -6 to 6
- sector_class: int32 [768], P('blk'), may hold values from 1 to 4
- left_env: bfloat16 [12288, 256, 256], P(('blk', 'mpo')), may hold values from -0.375 to 0.375
- right_env: bfloat16 [12288, 256, 256], P(('blk', 'mpo')), may hold values from -0.375 to 0.375
- term_source: int32 [12288], P(('blk', 'mpo')), may hold values from 0 to 767, as said below
- term_target: int32 [12288], P(('blk', 'mpo')), may hold values from -1 to 3, as said below
Outputs:
- hpsi: float32 [768, 256, 256], P('blk', 'mpo')
The draws below stay inside these ranges and needn't reach their ends.
Inputs may be any that keep to these rules, and one draw needn't show every extreme that they name: `term_source`: slot t of owner b reads a sector within 4 sectors of the owner's own: between (b - 1) * 4 and (b + 2) * 4 - 1. `term_target`: every device has at least 8 live slots, and some device has all 16 slots live.
All inputs are finite; a program needn't handle non-finite values.
Results may differ from the reference program's by a relative error of at most 0.0029.
Values may be sent and summed in bfloat16 or wider, within the bound.
No kernel may reach another device: no remote copies, remote signals or barrier semaphores. Data moves between devices by JAX's collectives and lax.ppermute only.
A program may use at most 32 MiB of HBM per device.

```python
import jax
import jax.numpy as jnp
from jax import lax

B = 256
PS_DEV = 4
TERM_DEV = 16
NS = 768
SLOTS = 12288
N_BLK = 192
N_MPO = 4
DEVICES = 768


def term_tables(key):
    key_count, key_full, key_order, key_target, key_offset = jax.random.split(key, 5)
    counts = jax.random.randint(key_count, (DEVICES,), TERM_DEV // 2, TERM_DEV + 1)
    busiest = jax.random.randint(key_full, (), 0, DEVICES)
    counts = jnp.where(jnp.arange(DEVICES) == busiest, TERM_DEV, counts)
    order = jax.vmap(lambda one_key: jax.random.permutation(one_key, TERM_DEV))(jax.random.split(key_order, DEVICES))
    live_slot = order < counts[:, None]
    targets = jax.random.randint(key_target, (DEVICES, TERM_DEV), 0, PS_DEV)
    targets = jnp.where(live_slot, targets, -1)
    owners = (jnp.arange(DEVICES) // N_MPO)[:, None]
    offsets = jax.random.randint(key_offset, (DEVICES, TERM_DEV), -PS_DEV, 2 * PS_DEV)
    sources = jnp.clip(owners * PS_DEV + offsets, 0, NS - 1)
    return (sources.reshape(-1).astype(jnp.int32), targets.reshape(-1).astype(jnp.int32))


def draw_term_source(key, part):
    return term_tables(key)[0]


def draw_term_target(key, part):
    return term_tables(key)[1]


def with_ends(values, rng, smallest, high):
    longest = values.shape.index(max(values.shape))
    spots = []
    for shift in (0, 1):
        where = [jax.random.randint(jax.random.fold_in(rng, axis), (), 0, length) for axis, length in enumerate(values.shape)]
        where[longest] = (where[longest] + shift) % values.shape[longest]
        spots.append(tuple(where))
    return values.at[spots[0]].set(smallest).at[spots[1]].set(high)


def levels(stream_key, shape, shards, low, top_value):
    factor_of, own = 1.0, jax.random.fold_in(stream_key, 6)
    for position, blocks in shards:
        draws = jnp.exp(jax.random.uniform(jax.random.fold_in(own, position), (blocks,), jnp.float32, low / len(shards), top_value / len(shards)))
        factor_of = factor_of * jnp.repeat(draws, shape[position] // blocks).reshape([-1 if axis == position else 1 for axis in range(len(shape))])
    return factor_of


def centred(stream_key, extent, scale, bound, cuts=(), kind=jnp.bfloat16):
    entries = scale * jax.random.normal(stream_key, extent, jnp.float32)
    if cuts:
        entries = entries * levels(stream_key, extent, cuts, -0.22, 0.18)
    return jnp.clip(entries, -bound, bound).astype(kind)


def setup_inputs(seed: int = 0) -> dict:
    seeds = jax.random.split(jax.random.key(seed), 7)
    psi = centred(seeds[0], (NS, B, B), 1.0, 6.0, ((0, 192),))
    sector_class = with_ends(jax.random.randint(seeds[1], (NS,), 1, 5), jax.random.fold_in(seeds[1], 1), 1, 4).astype(jnp.int32)
    left_env = centred(seeds[2], (SLOTS, B, B), B ** -0.5, 0.375, ((0, 768),))
    right_env = centred(seeds[3], (SLOTS, B, B), B ** -0.5, 0.375, ((0, 768),))
    term_source = draw_term_source(jax.random.fold_in(seeds[6], 71), 0)
    term_target = draw_term_target(jax.random.fold_in(seeds[6], 71), 0)
    return dict(psi=psi, sector_class=sector_class, left_env=left_env, right_env=right_env, term_source=term_source, term_target=term_target)


def reference(psi, sector_class, left_env, right_env, term_source, term_target):
    row_index = jnp.arange(B, dtype=jnp.int32)
    live_rows = sector_class * (B // 4)
    keep_mask = (row_index[None, :, None] < live_rows[:, None, None]) & (row_index[None, None, :] < live_rows[:, None, None])
    masked = jnp.where(keep_mask, psi, jnp.zeros_like(psi))
    per_owner = N_MPO * TERM_DEV
    left_blocks = left_env.reshape(N_BLK, per_owner, B, B)
    right_blocks = right_env.reshape(N_BLK, per_owner, B, B)
    sources = term_source.reshape(N_BLK, per_owner)
    targets = term_target.reshape(N_BLK, per_owner)

    def owner_block(items):
        left_one, right_one, source_one, target_one = items
        picked = masked[source_one].astype(jnp.float32)
        left_product = jnp.einsum('tij,tjk->tik', left_one.astype(jnp.float32), picked).astype(jnp.bfloat16)
        second = jnp.einsum('tik,tlk->til', left_product.astype(jnp.float32), right_one.astype(jnp.float32))
        onehot = (target_one[None, :] == jnp.arange(PS_DEV, dtype=jnp.int32)[:, None]).astype(jnp.float32)
        return jnp.einsum('pt,til->pil', onehot, second, precision=lax.Precision.HIGHEST)

    sums = lax.map(owner_block, (left_blocks, right_blocks, sources, targets)).reshape(NS, B, B)
    return jnp.where(keep_mask, sums, jnp.zeros_like(sums))
```

```python
import jax
import jax.numpy as jnp
from jax import lax
from jax.experimental import pallas as pl
from jax.experimental.pallas import tpu as pltpu
from jax.sharding import PartitionSpec as P

SMEM = pl.BlockSpec(memory_space=pltpu.SMEM)
VMEM = pl.BlockSpec(memory_space=pltpu.VMEM)


def masked_block(block, live):
    rows = lax.broadcasted_iota(jnp.int32, block.shape, 0)
    cols = lax.broadcasted_iota(jnp.int32, block.shape, 1)
    return jnp.where((rows < live) & (cols < live), block, jnp.zeros_like(block))


def terms_kernel(
    source_ref, target_ref, own_class, pair_class, next_class,
    own_ref, pair_ref, next_ref, left_ref, right_ref, out_ref, window, total,
):
    slots, size, _ = left_ref.shape
    sectors = own_ref.shape[0]
    groups, _, part_rows, _ = out_ref.shape
    owner = lax.axis_index("blk")
    odd = lax.rem(owner, 2)
    quarter = size // 4
    for group, (classes, blocks) in enumerate(
        ((own_class, own_ref), (pair_class, pair_ref), (next_class, next_ref))
    ):
        for s in range(sectors):
            window[group * sectors + s] = masked_block(blocks[s], classes[s] * quarter)
    total[...] = jnp.zeros_like(total)
    for t in range(slots):
        offset = source_ref[t] - (owner - 1) * sectors
        side = offset // sectors
        group = jnp.where(side == 1, 0, jnp.where((side == 2) == (odd == 0), 1, 2))
        place = group * sectors + lax.rem(offset, sectors)
        product = jnp.dot(
            left_ref[t], window[place], preferred_element_type=jnp.float32
        ).astype(jnp.bfloat16)
        term = lax.dot_general(
            product, right_ref[t], (((1,), (1,)), ((), ())), preferred_element_type=jnp.float32
        )
        target = target_ref[t]
        total[jnp.where(target < 0, sectors, target)] += term
    for g in range(groups):
        for s in range(sectors):
            out_ref[g, s] = total[s, g * part_rows : (g + 1) * part_rows, :].astype(out_ref.dtype)


def sum_kernel(class_ref, parts_ref, out_ref):
    groups, sectors, part_rows, size = parts_ref.shape
    position = lax.axis_index("mpo")
    quarter = size // 4
    for s in range(sectors):
        live = class_ref[s] * quarter
        summed = parts_ref[0, s].astype(jnp.float32)
        for g in range(1, groups):
            summed += parts_ref[g, s].astype(jnp.float32)
        rows = position * part_rows + lax.broadcasted_iota(jnp.int32, summed.shape, 0)
        cols = lax.broadcasted_iota(jnp.int32, summed.shape, 1)
        out_ref[s] = jnp.where((rows < live) & (cols < live), summed, 0.0)


def body(psi, sector_class, left_env, right_env, term_source, term_target):
    sectors, size, _ = psi.shape
    slots = left_env.shape[0]
    owners = lax.axis_size("blk")
    groups = lax.axis_size("mpo")
    part_rows = size // groups
    same_chip = [(i, i ^ 1) for i in range(owners)]
    next_chip = [(i, (i - 1 if i % 2 == 0 else i + 1) % owners) for i in range(owners)]
    following = lax.ppermute(psi, "blk", next_chip)
    pair = lax.ppermute(psi, "blk", same_chip)
    next_class = lax.ppermute(sector_class, "blk", next_chip)
    pair_class = lax.ppermute(sector_class, "blk", same_chip)
    keep = lambda x: pltpu.with_memory_space_constraint(x, pltpu.VMEM)
    parts = pl.pallas_call(
        terms_kernel,
        out_shape=jax.ShapeDtypeStruct((groups, sectors, part_rows, size), jnp.bfloat16),
        in_specs=[SMEM] * 5 + [VMEM] * 5,
        out_specs=VMEM,
        scratch_shapes=[
            pltpu.VMEM((3 * sectors, size, size), jnp.bfloat16),
            pltpu.VMEM((sectors + 1, size, size), jnp.float32),
        ],
        compiler_params=pltpu.CompilerParams(vmem_limit_bytes=24 * 2**20),
        cost_estimate=pl.CostEstimate(
            flops=4 * slots * size**3, bytes_accessed=4 * slots * size**2, transcendentals=0
        ),
        name="terms",
    )(
        term_source, term_target, sector_class, pair_class, next_class,
        keep(psi), keep(pair), keep(following), keep(left_env), keep(right_env),
    )
    received = lax.all_to_all(parts, "mpo", 0, 0)
    return pl.pallas_call(
        sum_kernel,
        out_shape=jax.ShapeDtypeStruct((sectors, part_rows, size), jnp.float32),
        in_specs=[SMEM, VMEM],
        out_specs=VMEM,
        name="sums",
    )(sector_class, received)


def solution(mesh):
    placed = (
        P("blk", None, None),
        P("blk"),
        P(("blk", "mpo"), None, None),
        P(("blk", "mpo"), None, None),
        P(("blk", "mpo")),
        P(("blk", "mpo")),
    )
    return jax.shard_map(
        body, mesh=mesh, in_specs=placed, out_specs=P("blk", "mpo", None), check_vma=False
    )
```

```python
import jax
import jax.numpy as jnp
from jax import lax
from jax.experimental import pallas as pl
from jax.experimental.pallas import tpu as pltpu
from jax.sharding import PartitionSpec as P

SMEM = pl.BlockSpec(memory_space=pltpu.SMEM)
VMEM = pl.BlockSpec(memory_space=pltpu.VMEM)
ANY = pl.BlockSpec(memory_space=pl.ANY)
UNROLL = 4


def in_vmem(x):
    return pltpu.with_memory_space_constraint(x, pltpu.VMEM)


def in_hbm(x):
    return pltpu.with_memory_space_constraint(x, pltpu.HBM)


def in_smem(x):
    return pltpu.with_memory_space_constraint(x, pltpu.SMEM)


def live_entries(shape, first_row, live):
    rows = first_row + lax.broadcasted_iota(jnp.int32, shape, 0)
    cols = lax.broadcasted_iota(jnp.int32, shape, 1)
    return (rows < live) & (cols < live)


def mask_kernel(class_hbm, psi_hbm, out_ref, classes, psi, class_sem, psi_sems):
    sectors, size, _ = psi.shape
    quarter = size // 4
    load_class = pltpu.make_async_copy(class_hbm, classes, class_sem)
    load_class.start()
    loads = []
    for s in range(sectors):
        loads.append(pltpu.make_async_copy(psi_hbm.at[s], psi.at[s], psi_sems.at[s]))
        loads[s].start()
    load_class.wait()
    cols = lax.broadcasted_iota(jnp.int32, (quarter, size), 1)
    for s in range(sectors):
        loads[s].wait()
        for q in range(4):
            rows = slice(q * quarter, (q + 1) * quarter)
            live = jnp.where(q < classes[s], classes[s] * quarter, 0)
            out_ref[s, rows, :] = jnp.where(cols < live, psi[s, rows, :], 0.0).astype(psi.dtype)


def fill_queue(queue, chosen, source_ref, target_ref):
    slots = source_ref.shape[0]
    for t in range(slots):
        queue[t] = 0
    count = jnp.int32(0)
    for t in range(slots):
        take = jnp.logical_and(target_ref[t] >= 0, chosen(source_ref[t]))
        queue[count] = jnp.where(take, t, 0)
        count += take.astype(jnp.int32)
    queue[slots] = count


def add_terms(queue, block_of, target_ref, left_ref, right_ref, total):
    slots = left_ref.shape[0]
    sectors = total.shape[0] - 1
    count = queue[slots]

    def step(i, carry):
        for j in range(UNROLL):
            n = i * UNROLL + j
            t = queue[n]
            product = jnp.dot(
                left_ref[t], block_of(t), preferred_element_type=jnp.float32
            ).astype(jnp.bfloat16)
            term = lax.dot_general(
                product, right_ref[t], (((1,), (1,)), ((), ())), preferred_element_type=jnp.float32
            )
            total[jnp.where(n < count, target_ref[t], sectors)] += term
        return carry

    lax.fori_loop(0, (count + UNROLL - 1) // UNROLL, step, 0)


def own_kernel(
    class_hbm, source_hbm, target_hbm, left_hbm, right_hbm, own_ref,
    total, left_ref, right_ref, keep_ref, copy_ref, target_ref, place_ref, others,
    classes, source_ref, queue, small_sems, left_sems, right_sems,
):
    slots, size, _ = left_ref.shape
    sectors, part_rows, _ = keep_ref.shape
    first = lax.axis_index("blk") * sectors
    chip_first = lax.axis_index("blk") // 2 * 2 * sectors
    small = [
        pltpu.make_async_copy(a, b, small_sems.at[i])
        for i, (a, b) in enumerate(
            ((source_hbm, source_ref), (target_hbm, target_ref), (class_hbm, classes))
        )
    ]
    large = []
    for t in range(slots):
        large.append(pltpu.make_async_copy(left_hbm.at[t], left_ref.at[t], left_sems.at[t]))
        large.append(pltpu.make_async_copy(right_hbm.at[t], right_ref.at[t], right_sems.at[t]))
    for copy in small + large:
        copy.start()
    copy_ref[...] = own_ref[...]
    total[...] = jnp.zeros_like(total)
    for copy in small:
        copy.wait()
    first_row = lax.axis_index("mpo") * part_rows
    for s in range(sectors):
        keep_ref[s] = live_entries(
            (part_rows, size), first_row, classes[s] * (size // 4)
        ).astype(jnp.float32)

    def is_own(source):
        return jnp.logical_and(source >= first, source < first + sectors)

    fill_queue(queue, is_own, source_ref, target_ref)
    fill_queue(others, lambda source: jnp.logical_not(is_own(source)), source_ref, target_ref)
    for t in range(slots):
        source = source_ref[t]
        near = jnp.logical_and(source >= chip_first, source < chip_first + 2 * sectors)
        place_ref[t] = lax.rem(source, sectors) + jnp.where(near, 0, sectors)
    for copy in large:
        copy.wait()
    add_terms(
        queue, lambda t: own_ref[lax.rem(source_ref[t], sectors)], target_ref, left_ref, right_ref, total
    )


def other_kernel(
    place_ref, target_ref, others, pair_ref, next_ref, given, left_ref, right_ref,
    parts_ref, total, window,
):
    groups, sectors, part_rows, _ = parts_ref.shape
    total[...] = given[...]
    window[:sectors] = pair_ref[...]
    window[sectors:] = next_ref[...]
    add_terms(others, lambda t: window[place_ref[t]], target_ref, left_ref, right_ref, total)
    for g in range(groups):
        for s in range(sectors):
            parts_ref[g, s] = total[s, g * part_rows : (g + 1) * part_rows, :].astype(
                parts_ref.dtype
            )


def body(psi, sector_class, left_env, right_env, term_source, term_target):
    sectors, size, _ = psi.shape
    slots = left_env.shape[0]
    owners = lax.axis_size("blk")
    groups = lax.axis_size("mpo")
    part_rows = size // groups
    same_chip = [(i, i ^ 1) for i in range(owners)]
    next_chip = [(i, i - 1 if i % 2 == 0 else i + 1) for i in range(1, owners - 1)]
    DMA = pltpu.SemaphoreType.DMA
    masked = pl.pallas_call(
        mask_kernel,
        out_shape=pltpu.VMEM(psi.shape, psi.dtype),
        in_specs=[ANY, ANY],
        out_specs=VMEM,
        scratch_shapes=[
            pltpu.SMEM((sectors,), jnp.int32),
            pltpu.VMEM(psi.shape, psi.dtype),
            DMA,
            DMA((sectors,)),
        ],
        name="masked",
    )(in_hbm(sector_class), in_hbm(psi))
    following = lax.ppermute(masked, "blk", next_chip)
    total, left, right, keep, copied, target, place, others = pl.pallas_call(
        own_kernel,
        out_shape=(
            pltpu.VMEM((sectors + 1, size, size), jnp.float32),
            pltpu.VMEM(left_env.shape, left_env.dtype),
            pltpu.VMEM(right_env.shape, right_env.dtype),
            pltpu.VMEM((sectors, part_rows, size), jnp.float32),
            pltpu.VMEM(psi.shape, psi.dtype),
            pltpu.SMEM((slots,), jnp.int32), pltpu.SMEM((slots,), jnp.int32), pltpu.SMEM((slots + 1,), jnp.int32),
        ),
        in_specs=[ANY] * 5 + [VMEM],
        out_specs=(VMEM,) * 5 + (SMEM,) * 3,
        scratch_shapes=[
            pltpu.SMEM((sectors,), jnp.int32),
            pltpu.SMEM((slots,), jnp.int32),
            pltpu.SMEM((slots + 1,), jnp.int32),
            DMA((3,)), DMA((slots,)), DMA((slots,)),
        ],
        compiler_params=pltpu.CompilerParams(vmem_limit_bytes=24 * 2**20),
        cost_estimate=pl.CostEstimate(
            flops=3 * slots * size**3, bytes_accessed=4 * slots * size**2, transcendentals=0
        ),
        name="own_terms",
    )(
        in_hbm(sector_class), in_hbm(term_source), in_hbm(term_target), in_hbm(left_env),
        in_hbm(right_env), in_vmem(masked),
    )
    pair = lax.ppermute(copied, "blk", same_chip)
    parts = pl.pallas_call(
        other_kernel,
        out_shape=pltpu.VMEM((groups, sectors, part_rows, size), jnp.bfloat16),
        in_specs=[SMEM] * 3 + [VMEM] * 5,
        out_specs=VMEM,
        scratch_shapes=[
            pltpu.VMEM((sectors + 1, size, size), jnp.float32),
            pltpu.VMEM((2 * sectors, size, size), jnp.bfloat16),
        ],
        compiler_params=pltpu.CompilerParams(vmem_limit_bytes=24 * 2**20),
        cost_estimate=pl.CostEstimate(
            flops=2 * slots * size**3, bytes_accessed=2 * slots * size**2, transcendentals=0
        ),
        name="other_terms",
    )(
        in_smem(place), in_smem(target), in_smem(others), in_vmem(pair), in_vmem(following), in_vmem(total),
        in_vmem(left), in_vmem(right),
    )
    received = lax.all_to_all(parts, "mpo", 0, 0)
    summed = received[0].astype(jnp.float32)
    for g in range(1, groups):
        summed += received[g].astype(jnp.float32)
    return jnp.where(keep != 0, summed, 0.0)


def solution(mesh):
    placed = (
        P("blk", None, None),
        P("blk"),
        P(("blk", "mpo"), None, None),
        P(("blk", "mpo"), None, None),
        P(("blk", "mpo")),
        P(("blk", "mpo")),
    )
    return jax.shard_map(
        body, mesh=mesh, in_specs=placed, out_specs=P("blk", "mpo", None), check_vma=False
    )
```

```python
import jax
import jax.numpy as jnp
from jax import lax
from jax.experimental import pallas as pl
from jax.experimental.pallas import tpu as pltpu
from jax.sharding import PartitionSpec as P

SMEM = pl.BlockSpec(memory_space=pltpu.SMEM)
VMEM = pl.BlockSpec(memory_space=pltpu.VMEM)
ANY = pl.BlockSpec(memory_space=pl.ANY)
DMA = pltpu.SemaphoreType.DMA
TOGETHER = 4


def in_vmem(x):
    return pltpu.with_memory_space_constraint(x, pltpu.VMEM)


def in_hbm(x):
    return pltpu.with_memory_space_constraint(x, pltpu.HBM)


def in_smem(x):
    return pltpu.with_memory_space_constraint(x, pltpu.SMEM)


def mask_rows(block, sector_class):
    size = block.shape[0]
    quarter = size // 4
    cols = lax.broadcasted_iota(jnp.int32, (quarter, size), 1)
    pieces = []
    for q in range(4):
        live = jnp.where(q < sector_class, sector_class * quarter, 0)
        piece = block[q * quarter : (q + 1) * quarter]
        pieces.append(jnp.where(cols < live, piece, jnp.zeros_like(piece)))
    return jnp.concatenate(pieces, axis=0)


def fill_queue(queue, chosen, source_ref, target_ref):
    slots = source_ref.shape[0]
    for t in range(slots):
        queue[t] = 0
    count = jnp.int32(0)
    for t in range(slots):
        take = jnp.logical_and(target_ref[t] >= 0, chosen(source_ref[t]))
        queue[count] = jnp.where(take, t, 0)
        count += take.astype(jnp.int32)
    queue[slots] = count


def add_together(n_first, together, queue, block_of, target_ref, left_ref, right_ref, total):
    sectors = total.shape[0] - 1
    count = queue[queue.shape[0] - 1]
    places = [n_first + j for j in range(together)]
    picked = [queue[n] for n in places]
    products = [
        jnp.dot(left_ref[t], block_of(t), preferred_element_type=jnp.float32).astype(jnp.bfloat16)
        for t in picked
    ]
    terms = [
        lax.dot_general(
            product, right_ref[t], (((1,), (1,)), ((), ())), preferred_element_type=jnp.float32
        )
        for product, t in zip(products, picked)
    ]
    for n, t, term in zip(places, picked, terms):
        total[jnp.where(n < count, target_ref[t], sectors)] += term


def add_terms(queue, block_of, target_ref, left_ref, right_ref, total, first=0):
    refs = (queue, block_of, target_ref, left_ref, right_ref, total)
    count = queue[queue.shape[0] - 1]
    if first:
        add_together(0, first, *refs)

    def step(i, carry):
        add_together(first + i * TOGETHER, TOGETHER, *refs)
        return carry

    rest = jnp.maximum(count - first, 0)
    lax.fori_loop(0, (rest + TOGETHER - 1) // TOGETHER, step, 0)


def load_terms(
    hbm, own_ref, total, left_ref, right_ref, target_ref, place_ref, others,
    source_ref, queue, small_sems, left_sems, right_sems,
):
    source_hbm, target_hbm, left_hbm, right_hbm = hbm
    slots, size, _ = left_ref.shape
    sectors = own_ref.shape[0]
    first = lax.axis_index("blk") * sectors
    chip_first = lax.axis_index("blk") // 2 * 2 * sectors
    small = [
        pltpu.make_async_copy(a, b, small_sems.at[i])
        for i, (a, b) in enumerate(((source_hbm, source_ref), (target_hbm, target_ref)))
    ]
    large = []
    for t in range(slots):
        large.append(pltpu.make_async_copy(left_hbm.at[t], left_ref.at[t], left_sems.at[t]))
        large.append(pltpu.make_async_copy(right_hbm.at[t], right_ref.at[t], right_sems.at[t]))
    for copy in small + large:
        copy.start()
    total[...] = jnp.zeros_like(total)
    for copy in small:
        copy.wait()
    def is_own(source):
        return jnp.logical_and(source >= first, source < first + sectors)

    fill_queue(queue, is_own, source_ref, target_ref)
    fill_queue(others, lambda source: jnp.logical_not(is_own(source)), source_ref, target_ref)
    for t in range(slots):
        near = jnp.logical_and(
            source_ref[t] >= chip_first, source_ref[t] < chip_first + 2 * sectors
        )
        place_ref[t] = lax.rem(source_ref[t], sectors) + jnp.where(near, 0, sectors)
    for copy in large:
        copy.wait()
    add_terms(
        queue,
        lambda t: own_ref[lax.rem(place_ref[t], sectors)],
        target_ref, left_ref, right_ref, total,
    )


def early_kernel(
    class_hbm, psi_hbm, source_hbm, target_hbm, left_hbm, right_hbm,
    masked_ref, class_ref, total, left_ref, right_ref, target_ref, place_ref, others,
    psi_ref, source_ref, queue, class_sem, psi_sems, small_sems, left_sems, right_sems,
):
    sectors = psi_ref.shape[0]
    load_class = pltpu.make_async_copy(class_hbm, class_ref, class_sem)
    blocks = [
        pltpu.make_async_copy(psi_hbm.at[s], psi_ref.at[s], psi_sems.at[s]) for s in range(sectors)
    ]
    load_class.start()
    for copy in blocks:
        copy.start()
    load_class.wait()
    for s in range(sectors):
        blocks[s].wait()
        masked_ref[s] = mask_rows(psi_ref[s], class_ref[s])

    @pl.when(lax.rem(lax.axis_index("blk"), 2) == 0)
    def _():
        load_terms(
            (source_hbm, target_hbm, left_hbm, right_hbm),
            masked_ref, total, left_ref, right_ref, target_ref, place_ref, others,
            source_ref, queue, small_sems, left_sems, right_sems,
        )


def late_kernel(
    source_hbm, target_hbm, left_hbm, right_hbm, own_ref, classes,
    copy_ref, keep_ref, total, left_ref, right_ref, target_ref, place_ref, others,
    source_ref, queue, small_sems, left_sems, right_sems,
):
    sectors, part_rows, size = keep_ref.shape
    copy_ref[...] = own_ref[...]
    first_row = lax.axis_index("mpo") * part_rows
    rows = first_row + lax.broadcasted_iota(jnp.int32, (part_rows, size), 0)
    cols = lax.broadcasted_iota(jnp.int32, (part_rows, size), 1)
    for s in range(sectors):
        live = classes[s] * (size // 4)
        keep_ref[s] = ((rows < live) & (cols < live)).astype(jnp.float32)

    @pl.when(lax.rem(lax.axis_index("blk"), 2) == 1)
    def _():
        load_terms(
            (source_hbm, target_hbm, left_hbm, right_hbm),
            own_ref, total, left_ref, right_ref, target_ref, place_ref, others,
            source_ref, queue, small_sems, left_sems, right_sems,
        )


def other_kernel(
    even_target, even_place, even_others, odd_target, odd_place, odd_others, pair_ref, next_ref,
    even_given, odd_given, even_left, even_right, odd_left, odd_right,
    parts_ref, even_total, odd_total,
):
    groups, sectors, part_rows, _ = parts_ref.shape
    odd = lax.rem(lax.axis_index("blk"), 2)

    def finish(place_ref, target_ref, others, left_ref, right_ref, total):
        def block_of(t):
            at = lax.rem(place_ref[t], sectors)
            return jnp.where(place_ref[t] < sectors, pair_ref[at], next_ref[at])

        add_terms(others, block_of, target_ref, left_ref, right_ref, total, 8)
        for g in range(groups):
            for s in range(sectors):
                parts_ref[g, s] = total[s, g * part_rows : (g + 1) * part_rows, :].astype(
                    parts_ref.dtype
                )

    @pl.when(odd == 0)
    def _():
        finish(even_place, even_target, even_others, even_left, even_right, even_total)

    @pl.when(odd == 1)
    def _():
        finish(odd_place, odd_target, odd_others, odd_left, odd_right, odd_total)


def body(psi, sector_class, left_env, right_env, term_source, term_target):
    sectors, size, _ = psi.shape
    slots = left_env.shape[0]
    owners = lax.axis_size("blk")
    groups = lax.axis_size("mpo")
    part_rows = size // groups
    same_chip = [(i, i ^ 1) for i in range(owners)]
    next_chip = [(i, i - 1 if i % 2 == 0 else i + 1) for i in range(1, owners - 1)]
    params = pltpu.CompilerParams(vmem_limit_bytes=24 * 2**20)
    sums = pltpu.VMEM((sectors + 1, size, size), jnp.float32)
    numbers = pltpu.SMEM((slots,), jnp.int32)
    queue = pltpu.SMEM((slots + 1,), jnp.int32)
    sector_blocks = pltpu.VMEM(psi.shape, psi.dtype)
    loaded = (
        sums,
        pltpu.VMEM(left_env.shape, left_env.dtype),
        pltpu.VMEM(right_env.shape, right_env.dtype),
        numbers, numbers, queue,
    )
    loaded_specs = (VMEM,) * 3 + (SMEM,) * 3
    load_scratch = [numbers, queue]
    load_sems = [DMA((2,)), DMA((slots,)), DMA((slots,))]
    tables = tuple(in_hbm(x) for x in (term_source, term_target, left_env, right_env))

    def cost(share):
        return pl.CostEstimate(
            flops=int(4 * slots * size**3 * share),
            bytes_accessed=int(4 * slots * size**2 * share),
            transcendentals=0,
        )

    masked, classes, *even = pl.pallas_call(
        early_kernel,
        out_shape=(sector_blocks, pltpu.SMEM((sectors,), jnp.int32), *loaded),
        in_specs=[ANY] * 6,
        out_specs=(VMEM, SMEM, *loaded_specs),
        scratch_shapes=[sector_blocks, *load_scratch, DMA, DMA((sectors,)), *load_sems],
        compiler_params=params,
        name="early_terms",
    )(in_hbm(sector_class), in_hbm(psi), *tables)
    following = lax.ppermute(masked, "blk", next_chip)
    copied, keep, *odd = pl.pallas_call(
        late_kernel,
        out_shape=(sector_blocks, pltpu.VMEM((sectors, part_rows, size), jnp.float32), *loaded),
        in_specs=[ANY] * 4 + [VMEM, SMEM],
        out_specs=(VMEM, VMEM, *loaded_specs),
        scratch_shapes=[*load_scratch, *load_sems],
        compiler_params=params,
        cost_estimate=cost(1),
        name="late_terms",
    )(*tables, in_vmem(masked), in_smem(classes))
    pair = lax.ppermute(copied, "blk", same_chip)
    even_total, even_left, even_right, *even_lists = even
    odd_total, odd_left, odd_right, *odd_lists = odd
    parts, _, _ = pl.pallas_call(
        other_kernel,
        out_shape=(
            pltpu.VMEM((groups, sectors, part_rows, size), jnp.bfloat16), sums, sums,
        ),
        in_specs=[SMEM] * 6 + [VMEM] * 8,
        out_specs=(VMEM,) * 3,
        input_output_aliases={8: 1, 9: 2},
        compiler_params=params,
        cost_estimate=cost(0.5),
        name="other_terms",
    )(
        *(in_smem(x) for x in (*even_lists, *odd_lists)),
        *(in_vmem(x) for x in (pair, following, even_total, odd_total)),
        *(in_vmem(x) for x in (even_left, even_right, odd_left, odd_right)),
    )
    received = lax.all_to_all(parts, "mpo", 0, 0)
    summed = received[0].astype(jnp.float32)
    for g in range(1, groups):
        summed += received[g].astype(jnp.float32)
    return jnp.where(keep != 0, summed, 0.0)


def solution(mesh):
    placed = (
        P("blk", None, None),
        P("blk"),
        P(("blk", "mpo"), None, None),
        P(("blk", "mpo"), None, None),
        P(("blk", "mpo")),
        P(("blk", "mpo")),
    )
    return jax.shard_map(
        body, mesh=mesh, in_specs=placed, out_specs=P("blk", "mpo", None), check_vma=False
    )
```

```python
import jax
import jax.numpy as jnp
from jax import lax
from jax.experimental import pallas as pl
from jax.experimental.pallas import tpu as pltpu
from jax.sharding import PartitionSpec as P

SMEM = pl.BlockSpec(memory_space=pltpu.SMEM)
VMEM = pl.BlockSpec(memory_space=pltpu.VMEM)
ANY = pl.BlockSpec(memory_space=pl.ANY)
DMA = pltpu.SemaphoreType.DMA
TOGETHER = 4
TILE_ROWS = 16


def in_vmem(x):
    return pltpu.with_memory_space_constraint(x, pltpu.VMEM)


def in_hbm(x):
    return pltpu.with_memory_space_constraint(x, pltpu.HBM)


def in_smem(x):
    return pltpu.with_memory_space_constraint(x, pltpu.SMEM)


def mask_rows(block, sector_class):
    size = block.shape[0]
    quarter = size // 4
    cols = lax.broadcasted_iota(jnp.int32, (TILE_ROWS, size), 1)
    keep = (cols < sector_class * quarter).astype(block.dtype)
    pieces = []
    for q in range(4):
        rows = keep * jnp.where(q < sector_class, 1.0, 0.0).astype(block.dtype)
        for r in range(0, quarter, TILE_ROWS):
            first = q * quarter + r
            pieces.append(block[first : first + TILE_ROWS] * rows)
    return jnp.concatenate(pieces, axis=0)


def fill_queue(queue, chosen, source_ref, target_ref):
    slots = source_ref.shape[0]
    for t in range(slots):
        queue[t] = 0
    count = jnp.int32(0)
    for t in range(slots):
        take = jnp.logical_and(target_ref[t] >= 0, chosen(source_ref[t]))
        queue[count] = jnp.where(take, t, 0)
        count += take.astype(jnp.int32)
    queue[slots] = count


def add_together(n_first, together, queue, block_of, target_ref, left_ref, right_ref, total):
    sectors = total.shape[0] - 1
    count = queue[queue.shape[0] - 1]
    places = [n_first + j for j in range(together)]
    picked = [queue[n] for n in places]
    products = [
        jnp.dot(left_ref[t], block_of(t), preferred_element_type=jnp.float32).astype(jnp.bfloat16)
        for t in picked
    ]
    terms = [
        lax.dot_general(
            product, right_ref[t], (((1,), (1,)), ((), ())), preferred_element_type=jnp.float32
        )
        for product, t in zip(products, picked)
    ]
    for n, t, term in zip(places, picked, terms):
        total[jnp.where(n < count, target_ref[t], sectors)] += term


def add_terms(queue, block_of, target_ref, left_ref, right_ref, total, first=0):
    refs = (queue, block_of, target_ref, left_ref, right_ref, total)
    count = queue[queue.shape[0] - 1]
    if first:
        add_together(0, first, *refs)

    def step(i, carry):
        add_together(first + i * TOGETHER, TOGETHER, *refs)
        return carry

    rest = jnp.maximum(count - first, 0)
    lax.fori_loop(0, (rest + TOGETHER - 1) // TOGETHER, step, 0)


def load_terms(
    hbm, own_ref, total, left_ref, right_ref, target_ref, place_ref, pair_queue, next_queue,
    source_ref, queue, small_sems, env_sems,
):
    source_hbm, target_hbm, left_hbm, right_hbm = hbm
    slots, size, _ = left_ref.shape
    sectors = total.shape[0] - 1
    first = lax.axis_index("blk") * sectors
    chip_first = lax.axis_index("blk") // 2 * 2 * sectors
    small = [
        pltpu.make_async_copy(a, b, small_sems.at[i])
        for i, (a, b) in enumerate(((source_hbm, source_ref), (target_hbm, target_ref)))
    ]
    piece = slots // 4
    whole = []
    for copy in small:
        copy.start()
    for i, (a, b) in enumerate(((left_hbm, left_ref), (right_hbm, right_ref))):
        for t in range(0, slots, piece):
            part = pl.ds(t, piece)
            pltpu.make_async_copy(a.at[part], b.at[part], env_sems.at[i]).start()
        whole.append(pltpu.make_async_copy(a, b, env_sems.at[i]))
    total[...] = jnp.zeros_like(total)
    for copy in small:
        copy.wait()
    def is_own(source):
        return jnp.logical_and(source >= first, source < first + sectors)

    fill_queue(queue, is_own, source_ref, target_ref)
    def is_near(source):
        return jnp.logical_and(source >= chip_first, source < chip_first + 2 * sectors)

    fill_queue(
        pair_queue,
        lambda source: jnp.logical_and(is_near(source), jnp.logical_not(is_own(source))),
        source_ref,
        target_ref,
    )
    fill_queue(next_queue, lambda source: jnp.logical_not(is_near(source)), source_ref, target_ref)
    for t in range(slots):
        place_ref[t] = lax.rem(source_ref[t], sectors)
    for copy in whole:
        copy.wait()
    add_terms(
        queue,
        lambda t: own_ref[pl.ds(pl.multiple_of(place_ref[t] * size, size), size), :],
        target_ref, left_ref, right_ref, total,
    )


def mask_kernel(class_hbm, psi_hbm, masked_ref, class_ref, psi_ref, class_sem, psi_sem):
    sectors, size, _ = psi_ref.shape
    load_class = pltpu.make_async_copy(class_hbm, class_ref, class_sem)
    load_psi = pltpu.make_async_copy(psi_hbm, psi_ref, psi_sem)
    load_class.start()
    load_psi.start()
    masked_ref[sectors * size :] = jnp.zeros((TILE_ROWS, size), masked_ref.dtype)
    load_class.wait()
    load_psi.wait()
    for s in range(sectors):
        masked_ref[s * size : (s + 1) * size] = mask_rows(psi_ref[s], class_ref[s])


def early_kernel(
    source_hbm, target_hbm, left_hbm, right_hbm, given_ref,
    masked_ref, total, left_ref, right_ref, target_ref, place_ref, pair_queue, next_queue,
    source_ref, queue, small_sems, env_sems,
):
    @pl.when(lax.rem(lax.axis_index("blk"), 2) == 0)
    def _():
        load_terms(
            (source_hbm, target_hbm, left_hbm, right_hbm),
            masked_ref, total, left_ref, right_ref, target_ref, place_ref, pair_queue, next_queue,
            source_ref, queue, small_sems, env_sems,
        )


def late_kernel(
    source_hbm, target_hbm, left_hbm, right_hbm, own_ref, classes,
    copy_ref, keep_ref, total, left_ref, right_ref, target_ref, place_ref, pair_queue, next_queue,
    source_ref, queue, small_sems, env_sems,
):
    sectors, part_rows, size = keep_ref.shape
    for s in range(sectors):
        copy_ref[s] = own_ref[s * size : (s + 1) * size]
    first_row = lax.axis_index("mpo") * part_rows
    rows = first_row + lax.broadcasted_iota(jnp.int32, (part_rows, size), 0)
    cols = lax.broadcasted_iota(jnp.int32, (part_rows, size), 1)
    for s in range(sectors):
        live = classes[s] * (size // 4)
        keep_ref[s] = ((rows < live) & (cols < live)).astype(jnp.float32)

    @pl.when(lax.rem(lax.axis_index("blk"), 2) == 1)
    def _():
        load_terms(
            (source_hbm, target_hbm, left_hbm, right_hbm),
            own_ref, total, left_ref, right_ref, target_ref, place_ref, pair_queue, next_queue,
            source_ref, queue, small_sems, env_sems,
        )


def pair_kernel(
    even_target, even_place, even_queue, odd_target, odd_place, odd_queue, pair_ref,
    even_given, odd_given, even_left, even_right, odd_left, odd_right, even_total, odd_total,
):
    odd = lax.rem(lax.axis_index("blk"), 2)

    def add(place_ref, target_ref, queue, left_ref, right_ref, total):
        add_terms(queue, lambda t: pair_ref[place_ref[t]], target_ref, left_ref, right_ref, total)

    @pl.when(odd == 0)
    def _():
        add(even_place, even_target, even_queue, even_left, even_right, even_total)

    @pl.when(odd == 1)
    def _():
        add(odd_place, odd_target, odd_queue, odd_left, odd_right, odd_total)


def next_kernel(
    even_target, even_place, even_queue, odd_target, odd_place, odd_queue, next_ref,
    even_given, odd_given, even_left, even_right, odd_left, odd_right,
    parts_ref, even_total, odd_total,
):
    groups, sectors, part_rows, size = parts_ref.shape
    odd = lax.rem(lax.axis_index("blk"), 2)

    def finish(place_ref, target_ref, queue, left_ref, right_ref, total):
        def block_of(t):
            return next_ref[pl.ds(pl.multiple_of(place_ref[t] * size, size), size), :]

        add_terms(queue, block_of, target_ref, left_ref, right_ref, total, 8)
        for g in range(groups):
            for s in range(sectors):
                parts_ref[g, s] = total[s, g * part_rows : (g + 1) * part_rows, :].astype(
                    parts_ref.dtype
                )

    @pl.when(odd == 0)
    def _():
        finish(even_place, even_target, even_queue, even_left, even_right, even_total)

    @pl.when(odd == 1)
    def _():
        finish(odd_place, odd_target, odd_queue, odd_left, odd_right, odd_total)


def body(psi, sector_class, left_env, right_env, term_source, term_target):
    sectors, size, _ = psi.shape
    slots = left_env.shape[0]
    owners = lax.axis_size("blk")
    groups = lax.axis_size("mpo")
    part_rows = size // groups
    same_chip = [(i, i ^ 1) for i in range(owners)]
    next_chip = [(i, i - 1 if i % 2 == 0 else i + 1) for i in range(1, owners - 1)]
    params = pltpu.CompilerParams(vmem_limit_bytes=24 * 2**20)
    sums = pltpu.VMEM((sectors + 1, size, size), jnp.float32)
    numbers = pltpu.SMEM((slots,), jnp.int32)
    queue = pltpu.SMEM((slots + 1,), jnp.int32)
    sector_blocks = pltpu.VMEM(psi.shape, psi.dtype)
    sent_rows = pltpu.VMEM((sectors * size + TILE_ROWS, size), psi.dtype)
    loaded = (
        sums,
        pltpu.VMEM(left_env.shape, left_env.dtype),
        pltpu.VMEM(right_env.shape, right_env.dtype),
        numbers, numbers, queue, queue,
    )
    loaded_specs = (VMEM,) * 3 + (SMEM,) * 4
    load_scratch = [numbers, queue]
    load_sems = [DMA((2,)), DMA((2,))]
    tables = tuple(in_hbm(x) for x in (term_source, term_target, left_env, right_env))

    def cost(share):
        return pl.CostEstimate(
            flops=int(4 * slots * size**3 * share),
            bytes_accessed=int(4 * slots * size**2 * share),
            transcendentals=0,
        )

    masked, classes = pl.pallas_call(
        mask_kernel,
        out_shape=(sent_rows, pltpu.SMEM((sectors,), jnp.int32)),
        in_specs=[ANY] * 2,
        out_specs=(VMEM, SMEM),
        scratch_shapes=[sector_blocks, DMA, DMA],
        compiler_params=params,
        name="masked",
    )(in_hbm(sector_class), in_hbm(psi))
    masked, *even = pl.pallas_call(
        early_kernel,
        out_shape=(sent_rows, *loaded),
        in_specs=[ANY] * 4 + [VMEM],
        out_specs=(VMEM, *loaded_specs),
        input_output_aliases={4: 0},
        scratch_shapes=[*load_scratch, *load_sems],
        compiler_params=params,
        name="early_terms",
    )(*tables, in_vmem(masked))
    following = lax.ppermute(masked, "blk", next_chip)
    copied, keep, *odd = pl.pallas_call(
        late_kernel,
        out_shape=(sector_blocks, pltpu.VMEM((sectors, part_rows, size), jnp.float32), *loaded),
        in_specs=[ANY] * 4 + [VMEM, SMEM],
        out_specs=(VMEM, VMEM, *loaded_specs),
        scratch_shapes=[*load_scratch, *load_sems],
        compiler_params=params,
        cost_estimate=cost(1),
        name="late_terms",
    )(*tables, in_vmem(masked), in_smem(classes))
    pair = lax.ppermute(copied, "blk", same_chip)
    even_total, even_left, even_right, even_target, even_place, even_pair, even_next = even
    odd_total, odd_left, odd_right, odd_target, odd_place, odd_pair, odd_next = odd
    envs = tuple(in_vmem(x) for x in (even_left, even_right, odd_left, odd_right))
    even_total, odd_total = pl.pallas_call(
        pair_kernel,
        out_shape=(sums, sums),
        in_specs=[SMEM] * 6 + [VMEM] * 7,
        out_specs=(VMEM,) * 2,
        input_output_aliases={7: 0, 8: 1},
        compiler_params=params,
        cost_estimate=cost(0.001),
        name="pair_terms",
    )(
        *(in_smem(x) for x in (even_target, even_place, even_pair)),
        *(in_smem(x) for x in (odd_target, odd_place, odd_pair)),
        *(in_vmem(x) for x in (pair, even_total, odd_total)),
        *envs,
    )
    parts, _, _ = pl.pallas_call(
        next_kernel,
        out_shape=(pltpu.VMEM((groups, sectors, part_rows, size), jnp.bfloat16), sums, sums),
        in_specs=[SMEM] * 6 + [VMEM] * 7,
        out_specs=(VMEM,) * 3,
        input_output_aliases={7: 1, 8: 2},
        compiler_params=params,
        cost_estimate=cost(0.5),
        name="next_terms",
    )(
        *(in_smem(x) for x in (even_target, even_place, even_next)),
        *(in_smem(x) for x in (odd_target, odd_place, odd_next)),
        *(in_vmem(x) for x in (following, even_total, odd_total)),
        *envs,
    )
    received = lax.all_to_all(parts, "mpo", 0, 0)
    summed = received[0].astype(jnp.float32)
    for g in range(1, groups):
        summed += received[g].astype(jnp.float32)
    return jnp.where(keep != 0, summed, 0.0)


def solution(mesh):
    placed = (
        P("blk", None, None),
        P("blk"),
        P(("blk", "mpo"), None, None),
        P(("blk", "mpo"), None, None),
        P(("blk", "mpo")),
        P(("blk", "mpo")),
    )
    return jax.shard_map(
        body, mesh=mesh, in_specs=placed, out_specs=P("blk", "mpo", None), check_vma=False
    )
```

```python
import jax
import jax.numpy as jnp
from jax import lax
from jax.experimental import pallas as pl
from jax.experimental.pallas import tpu as pltpu
from jax.sharding import PartitionSpec as P

SMEM = pl.BlockSpec(memory_space=pltpu.SMEM)
VMEM = pl.BlockSpec(memory_space=pltpu.VMEM)
ANY = pl.BlockSpec(memory_space=pl.ANY)
DMA = pltpu.SemaphoreType.DMA
TOGETHER = 4
TILE_ROWS = 16


def in_vmem(x):
    return pltpu.with_memory_space_constraint(x, pltpu.VMEM)


def in_hbm(x):
    return pltpu.with_memory_space_constraint(x, pltpu.HBM)


def in_smem(x):
    return pltpu.with_memory_space_constraint(x, pltpu.SMEM)


def mask_rows(block, sector_class):
    size = block.shape[0]
    quarter = size // 4
    cols = lax.broadcasted_iota(jnp.int32, (TILE_ROWS, size), 1)
    keep = (cols < sector_class * quarter).astype(block.dtype)
    pieces = []
    for q in range(4):
        rows = keep * jnp.where(q < sector_class, 1.0, 0.0).astype(block.dtype)
        for r in range(0, quarter, TILE_ROWS):
            first = q * quarter + r
            pieces.append(block[first : first + TILE_ROWS] * rows)
    return jnp.concatenate(pieces, axis=0)


def fill_queue(queue, chosen, source_ref, target_ref):
    slots = source_ref.shape[0]
    for t in range(slots):
        queue[t] = 0
    count = jnp.int32(0)
    for t in range(slots):
        take = jnp.logical_and(target_ref[t] >= 0, chosen(source_ref[t]))
        queue[count] = jnp.where(take, t, 0)
        count += take.astype(jnp.int32)
    queue[slots] = count


def add_together(n_first, together, queue, block_of, target_ref, left_ref, right_ref, total):
    sectors = total.shape[0] - 1
    count = queue[queue.shape[0] - 1]
    places = [n_first + j for j in range(together)]
    picked = [queue[n] for n in places]
    products = [
        jnp.dot(left_ref[t], block_of(t), preferred_element_type=jnp.float32).astype(jnp.bfloat16)
        for t in picked
    ]
    terms = [
        lax.dot_general(
            product, right_ref[t], (((1,), (1,)), ((), ())), preferred_element_type=jnp.float32
        )
        for product, t in zip(products, picked)
    ]
    for n, t, term in zip(places, picked, terms):
        total[jnp.where(n < count, target_ref[t], sectors)] += term


def add_terms(queue, block_of, target_ref, left_ref, right_ref, total, first=0, together=TOGETHER):
    refs = (queue, block_of, target_ref, left_ref, right_ref, total)
    count = queue[queue.shape[0] - 1]
    if first:
        add_together(0, first, *refs)

    def step(i, carry):
        add_together(first + i * together, together, *refs)
        return carry

    rest = jnp.maximum(count - first, 0)
    lax.fori_loop(0, (rest + together - 1) // together, step, 0)


def load_terms(
    hbm, own_ref, total, left_ref, right_ref, target_ref, place_ref, pair_queue, next_queue,
    source_ref, queue, small_sems, env_sems,
):
    source_hbm, target_hbm, left_hbm, right_hbm = hbm
    slots, size, _ = left_ref.shape
    sectors = total.shape[0] - 1
    first = lax.axis_index("blk") * sectors
    chip_first = lax.axis_index("blk") // 2 * 2 * sectors
    small = [
        pltpu.make_async_copy(a, b, small_sems.at[i])
        for i, (a, b) in enumerate(((source_hbm, source_ref), (target_hbm, target_ref)))
    ]
    piece = slots // 4
    whole = []
    for copy in small:
        copy.start()
    for i, (a, b) in enumerate(((left_hbm, left_ref), (right_hbm, right_ref))):
        for t in range(0, slots, piece):
            part = pl.ds(t, piece)
            pltpu.make_async_copy(a.at[part], b.at[part], env_sems.at[i]).start()
        whole.append(pltpu.make_async_copy(a, b, env_sems.at[i]))
    total[...] = jnp.zeros_like(total)
    for copy in small:
        copy.wait()
    def is_own(source):
        return jnp.logical_and(source >= first, source < first + sectors)

    fill_queue(queue, is_own, source_ref, target_ref)
    def is_near(source):
        return jnp.logical_and(source >= chip_first, source < chip_first + 2 * sectors)

    fill_queue(
        pair_queue,
        lambda source: jnp.logical_and(is_near(source), jnp.logical_not(is_own(source))),
        source_ref,
        target_ref,
    )
    fill_queue(next_queue, lambda source: jnp.logical_not(is_near(source)), source_ref, target_ref)
    for t in range(slots):
        place_ref[t] = lax.rem(source_ref[t], sectors)
    for copy in whole:
        copy.wait()
    add_terms(
        queue,
        lambda t: own_ref[pl.ds(pl.multiple_of(place_ref[t] * size, size), size), :],
        target_ref, left_ref, right_ref, total,
    )


def mask_kernel(class_hbm, psi_hbm, masked_ref, class_ref, psi_ref, class_sem, psi_sem):
    sectors, size, _ = psi_ref.shape
    load_class = pltpu.make_async_copy(class_hbm, class_ref, class_sem)
    load_psi = pltpu.make_async_copy(psi_hbm, psi_ref, psi_sem)
    load_class.start()
    load_psi.start()
    masked_ref[sectors * size :] = jnp.zeros((TILE_ROWS, size), masked_ref.dtype)
    load_class.wait()
    load_psi.wait()
    for s in range(sectors):
        masked_ref[s * size : (s + 1) * size] = mask_rows(psi_ref[s], class_ref[s])


def early_kernel(
    source_hbm, target_hbm, left_hbm, right_hbm, given_ref,
    masked_ref, total, left_ref, right_ref, target_ref, place_ref, pair_queue, next_queue,
    source_ref, queue, small_sems, env_sems,
):
    @pl.when(lax.rem(lax.axis_index("blk"), 2) == 0)
    def _():
        load_terms(
            (source_hbm, target_hbm, left_hbm, right_hbm),
            masked_ref, total, left_ref, right_ref, target_ref, place_ref, pair_queue, next_queue,
            source_ref, queue, small_sems, env_sems,
        )


def late_kernel(
    source_hbm, target_hbm, left_hbm, right_hbm, own_ref, classes,
    copy_ref, keep_ref, total, left_ref, right_ref, target_ref, place_ref, pair_queue, next_queue,
    source_ref, queue, small_sems, env_sems,
):
    sectors, part_rows, size = keep_ref.shape
    for s in range(sectors):
        copy_ref[s] = own_ref[s * size : (s + 1) * size]
    first_row = lax.axis_index("mpo") * part_rows
    rows = first_row + lax.broadcasted_iota(jnp.int32, (part_rows, size), 0)
    cols = lax.broadcasted_iota(jnp.int32, (part_rows, size), 1)
    for s in range(sectors):
        live = classes[s] * (size // 4)
        keep_ref[s] = ((rows < live) & (cols < live)).astype(jnp.float32)

    @pl.when(lax.rem(lax.axis_index("blk"), 2) == 1)
    def _():
        load_terms(
            (source_hbm, target_hbm, left_hbm, right_hbm),
            own_ref, total, left_ref, right_ref, target_ref, place_ref, pair_queue, next_queue,
            source_ref, queue, small_sems, env_sems,
        )


def pair_kernel(
    even_target, even_place, even_queue, odd_target, odd_place, odd_queue, pair_ref,
    even_given, odd_given, even_left, even_right, odd_left, odd_right, even_total, odd_total,
):
    odd = lax.rem(lax.axis_index("blk"), 2)

    def add(place_ref, target_ref, queue, left_ref, right_ref, total):
        add_terms(queue, lambda t: pair_ref[place_ref[t]], target_ref, left_ref, right_ref, total)

    @pl.when(odd == 0)
    def _():
        add(even_place, even_target, even_queue, even_left, even_right, even_total)

    @pl.when(odd == 1)
    def _():
        add(odd_place, odd_target, odd_queue, odd_left, odd_right, odd_total)


def next_kernel(
    even_target, even_place, even_queue, odd_target, odd_place, odd_queue, next_ref,
    even_given, odd_given, even_left, even_right, odd_left, odd_right,
    parts_ref, even_total, odd_total,
):
    groups, sectors, part_rows, size = parts_ref.shape
    odd = lax.rem(lax.axis_index("blk"), 2)

    def finish(place_ref, target_ref, queue, left_ref, right_ref, total):
        def block_of(t):
            return next_ref[pl.ds(pl.multiple_of(place_ref[t] * size, size), size), :]

        add_terms(queue, block_of, target_ref, left_ref, right_ref, total, 6, 2)
        for g in range(groups):
            for s in range(sectors):
                parts_ref[g, s] = total[s, g * part_rows : (g + 1) * part_rows, :].astype(
                    parts_ref.dtype
                )

    @pl.when(odd == 0)
    def _():
        finish(even_place, even_target, even_queue, even_left, even_right, even_total)

    @pl.when(odd == 1)
    def _():
        finish(odd_place, odd_target, odd_queue, odd_left, odd_right, odd_total)


def body(psi, sector_class, left_env, right_env, term_source, term_target):
    sectors, size, _ = psi.shape
    slots = left_env.shape[0]
    owners = lax.axis_size("blk")
    groups = lax.axis_size("mpo")
    part_rows = size // groups
    same_chip = [(i, i ^ 1) for i in range(owners)]
    next_chip = [(i, i - 1 if i % 2 == 0 else i + 1) for i in range(1, owners - 1)]
    params = pltpu.CompilerParams(vmem_limit_bytes=24 * 2**20)
    sums = pltpu.VMEM((sectors + 1, size, size), jnp.float32)
    numbers = pltpu.SMEM((slots,), jnp.int32)
    queue = pltpu.SMEM((slots + 1,), jnp.int32)
    sector_blocks = pltpu.VMEM(psi.shape, psi.dtype)
    sent_rows = pltpu.VMEM((sectors * size + TILE_ROWS, size), psi.dtype)
    loaded = (
        sums,
        pltpu.VMEM(left_env.shape, left_env.dtype),
        pltpu.VMEM(right_env.shape, right_env.dtype),
        numbers, numbers, queue, queue,
    )
    loaded_specs = (VMEM,) * 3 + (SMEM,) * 4
    load_scratch = [numbers, queue]
    load_sems = [DMA((2,)), DMA((2,))]
    tables = tuple(in_hbm(x) for x in (term_source, term_target, left_env, right_env))

    def cost(share):
        return pl.CostEstimate(
            flops=int(4 * slots * size**3 * share),
            bytes_accessed=int(4 * slots * size**2 * share),
            transcendentals=0,
        )

    masked, classes = pl.pallas_call(
        mask_kernel,
        out_shape=(sent_rows, pltpu.SMEM((sectors,), jnp.int32)),
        in_specs=[ANY] * 2,
        out_specs=(VMEM, SMEM),
        scratch_shapes=[sector_blocks, DMA, DMA],
        compiler_params=params,
        name="masked",
    )(in_hbm(sector_class), in_hbm(psi))
    masked, *even = pl.pallas_call(
        early_kernel,
        out_shape=(sent_rows, *loaded),
        in_specs=[ANY] * 4 + [VMEM],
        out_specs=(VMEM, *loaded_specs),
        input_output_aliases={4: 0},
        scratch_shapes=[*load_scratch, *load_sems],
        compiler_params=params,
        name="early_terms",
    )(*tables, in_vmem(masked))
    following = lax.ppermute(masked, "blk", next_chip)
    copied, keep, *odd = pl.pallas_call(
        late_kernel,
        out_shape=(sector_blocks, pltpu.VMEM((sectors, part_rows, size), jnp.float32), *loaded),
        in_specs=[ANY] * 4 + [VMEM, SMEM],
        out_specs=(VMEM, VMEM, *loaded_specs),
        scratch_shapes=[*load_scratch, *load_sems],
        compiler_params=params,
        cost_estimate=cost(1),
        name="late_terms",
    )(*tables, in_vmem(masked), in_smem(classes))
    pair = lax.ppermute(copied, "blk", same_chip)
    even_total, even_left, even_right, even_target, even_place, even_pair, even_next = even
    odd_total, odd_left, odd_right, odd_target, odd_place, odd_pair, odd_next = odd
    envs = tuple(in_vmem(x) for x in (even_left, even_right, odd_left, odd_right))
    even_total, odd_total = pl.pallas_call(
        pair_kernel,
        out_shape=(sums, sums),
        in_specs=[SMEM] * 6 + [VMEM] * 7,
        out_specs=(VMEM,) * 2,
        input_output_aliases={7: 0, 8: 1},
        compiler_params=params,
        cost_estimate=cost(0.001),
        name="pair_terms",
    )(
        *(in_smem(x) for x in (even_target, even_place, even_pair)),
        *(in_smem(x) for x in (odd_target, odd_place, odd_pair)),
        *(in_vmem(x) for x in (pair, even_total, odd_total)),
        *envs,
    )
    parts, _, _ = pl.pallas_call(
        next_kernel,
        out_shape=(pltpu.VMEM((groups, sectors, part_rows, size), jnp.bfloat16), sums, sums),
        in_specs=[SMEM] * 6 + [VMEM] * 7,
        out_specs=(VMEM,) * 3,
        input_output_aliases={7: 1, 8: 2},
        compiler_params=params,
        cost_estimate=cost(0.5),
        name="next_terms",
    )(
        *(in_smem(x) for x in (even_target, even_place, even_next)),
        *(in_smem(x) for x in (odd_target, odd_place, odd_next)),
        *(in_vmem(x) for x in (following, even_total, odd_total)),
        *envs,
    )
    received = lax.all_to_all(parts, "mpo", 0, 0)
    summed = received[0].astype(jnp.float32)
    for g in range(1, groups):
        summed += received[g].astype(jnp.float32)
    return jnp.where(keep != 0, summed, 0.0)


def solution(mesh):
    placed = (
        P("blk", None, None),
        P("blk"),
        P(("blk", "mpo"), None, None),
        P(("blk", "mpo"), None, None),
        P(("blk", "mpo")),
        P(("blk", "mpo")),
    )
    return jax.shard_map(
        body, mesh=mesh, in_specs=placed, out_specs=P("blk", "mpo", None), check_vma=False
    )
```

```python
import jax
import jax.numpy as jnp
from jax import lax
from jax.experimental import pallas as pl
from jax.experimental.pallas import tpu as pltpu
from jax.sharding import PartitionSpec as P

SMEM = pl.BlockSpec(memory_space=pltpu.SMEM)
VMEM = pl.BlockSpec(memory_space=pltpu.VMEM)
ANY = pl.BlockSpec(memory_space=pl.ANY)
DMA = pltpu.SemaphoreType.DMA
TOGETHER = 4
TILE_ROWS = 16


def in_vmem(x):
    return pltpu.with_memory_space_constraint(x, pltpu.VMEM)


def in_hbm(x):
    return pltpu.with_memory_space_constraint(x, pltpu.HBM)


def in_smem(x):
    return pltpu.with_memory_space_constraint(x, pltpu.SMEM)


def mask_rows(block, sector_class):
    size = block.shape[0]
    quarter = size // 4
    cols = lax.broadcasted_iota(jnp.int32, (TILE_ROWS, size), 1)
    keep = (cols < sector_class * quarter).astype(block.dtype)
    pieces = []
    for q in range(4):
        rows = keep * jnp.where(q < sector_class, 1.0, 0.0).astype(block.dtype)
        for r in range(0, quarter, TILE_ROWS):
            first = q * quarter + r
            pieces.append(block[first : first + TILE_ROWS] * rows)
    return jnp.concatenate(pieces, axis=0)


def fill_queue(queue, chosen, source_ref, target_ref):
    slots = source_ref.shape[0]
    for t in range(slots):
        queue[t] = 0
    count = jnp.int32(0)
    for t in range(slots):
        take = jnp.logical_and(target_ref[t] >= 0, chosen(source_ref[t]))
        queue[count] = jnp.where(take, t, 0)
        count += take.astype(jnp.int32)
    queue[slots] = count


def add_together(n_first, together, queue, block_of, target_ref, left_ref, right_ref, total):
    sectors = total.shape[0] - 1
    count = queue[queue.shape[0] - 1]
    places = [n_first + j for j in range(together)]
    picked = [queue[n] for n in places]
    products = [
        jnp.dot(left_ref[t], block_of(t), preferred_element_type=jnp.float32).astype(jnp.bfloat16)
        for t in picked
    ]
    terms = [
        lax.dot_general(
            product, right_ref[t], (((1,), (1,)), ((), ())), preferred_element_type=jnp.float32
        )
        for product, t in zip(products, picked)
    ]
    for n, t, term in zip(places, picked, terms):
        total[jnp.where(n < count, target_ref[t], sectors)] += term


def add_terms(queue, block_of, target_ref, left_ref, right_ref, total, first=0, together=TOGETHER):
    refs = (queue, block_of, target_ref, left_ref, right_ref, total)
    count = queue[queue.shape[0] - 1]
    if first:
        add_together(0, first, *refs)

    def step(i, carry):
        add_together(first + i * together, together, *refs)
        return carry

    rest = jnp.maximum(count - first, 0)
    lax.fori_loop(0, (rest + together - 1) // together, step, 0)


def load_terms(
    hbm, own_ref, total, left_ref, right_ref, target_ref, place_ref, pair_queue, next_queue,
    source_ref, queue, small_sems, env_sems,
):
    source_hbm, target_hbm, left_hbm, right_hbm = hbm
    slots, size, _ = left_ref.shape
    sectors = total.shape[0] - 1
    first = lax.axis_index("blk") * sectors
    chip_first = lax.axis_index("blk") // 2 * 2 * sectors
    small = [
        pltpu.make_async_copy(a, b, small_sems.at[i])
        for i, (a, b) in enumerate(((source_hbm, source_ref), (target_hbm, target_ref)))
    ]
    piece = slots // 4
    whole = []
    for copy in small:
        copy.start()
    for i, (a, b) in enumerate(((left_hbm, left_ref), (right_hbm, right_ref))):
        for t in range(0, slots, piece):
            part = pl.ds(t, piece)
            pltpu.make_async_copy(a.at[part], b.at[part], env_sems.at[i]).start()
        whole.append(pltpu.make_async_copy(a, b, env_sems.at[i]))
    total[...] = jnp.zeros_like(total)
    for copy in small:
        copy.wait()
    def is_own(source):
        return jnp.logical_and(source >= first, source < first + sectors)

    fill_queue(queue, is_own, source_ref, target_ref)
    def is_near(source):
        return jnp.logical_and(source >= chip_first, source < chip_first + 2 * sectors)

    fill_queue(
        pair_queue,
        lambda source: jnp.logical_and(is_near(source), jnp.logical_not(is_own(source))),
        source_ref,
        target_ref,
    )
    fill_queue(next_queue, lambda source: jnp.logical_not(is_near(source)), source_ref, target_ref)
    for t in range(slots):
        place_ref[t] = lax.rem(source_ref[t], sectors)
    for copy in whole:
        copy.wait()
    add_terms(
        queue,
        lambda t: own_ref[pl.ds(pl.multiple_of(place_ref[t] * size, size), size), :],
        target_ref, left_ref, right_ref, total,
    )


def mask_kernel(class_hbm, psi_hbm, masked_ref, class_ref, psi_ref, class_sem, psi_sem):
    sectors, size, _ = psi_ref.shape
    load_class = pltpu.make_async_copy(class_hbm, class_ref, class_sem)
    load_psi = pltpu.make_async_copy(psi_hbm, psi_ref, psi_sem)
    load_class.start()
    load_psi.start()
    masked_ref[sectors * size :] = jnp.zeros((TILE_ROWS, size), masked_ref.dtype)
    load_class.wait()
    load_psi.wait()
    for s in range(sectors):
        masked_ref[s * size : (s + 1) * size] = mask_rows(psi_ref[s], class_ref[s])


def early_kernel(
    source_hbm, target_hbm, left_hbm, right_hbm, given_ref,
    masked_ref, total, left_ref, right_ref, target_ref, place_ref, pair_queue, next_queue,
    source_ref, queue, small_sems, env_sems,
):
    @pl.when(lax.rem(lax.axis_index("blk"), 2) == 0)
    def _():
        load_terms(
            (source_hbm, target_hbm, left_hbm, right_hbm),
            masked_ref, total, left_ref, right_ref, target_ref, place_ref, pair_queue, next_queue,
            source_ref, queue, small_sems, env_sems,
        )


def late_kernel(
    source_hbm, target_hbm, left_hbm, right_hbm, own_ref, classes,
    copy_ref, keep_ref, total, left_ref, right_ref, target_ref, place_ref, pair_queue, next_queue,
    source_ref, queue, small_sems, env_sems,
):
    sectors, part_rows, size = keep_ref.shape
    for s in range(sectors):
        copy_ref[s] = own_ref[s * size : (s + 1) * size]
    first_row = lax.axis_index("mpo") * part_rows
    rows = first_row + lax.broadcasted_iota(jnp.int32, (part_rows, size), 0)
    cols = lax.broadcasted_iota(jnp.int32, (part_rows, size), 1)
    for s in range(sectors):
        live = classes[s] * (size // 4)
        keep_ref[s] = ((rows < live) & (cols < live)).astype(jnp.float32)

    @pl.when(lax.rem(lax.axis_index("blk"), 2) == 1)
    def _():
        load_terms(
            (source_hbm, target_hbm, left_hbm, right_hbm),
            own_ref, total, left_ref, right_ref, target_ref, place_ref, pair_queue, next_queue,
            source_ref, queue, small_sems, env_sems,
        )


def pair_kernel(
    even_target, even_place, even_queue, odd_target, odd_place, odd_queue, pair_ref,
    even_given, odd_given, even_left, even_right, odd_left, odd_right, even_total, odd_total,
):
    odd = lax.rem(lax.axis_index("blk"), 2)

    def add(place_ref, target_ref, queue, left_ref, right_ref, total):
        add_terms(queue, lambda t: pair_ref[place_ref[t]], target_ref, left_ref, right_ref, total)

    @pl.when(odd == 0)
    def _():
        add(even_place, even_target, even_queue, even_left, even_right, even_total)

    @pl.when(odd == 1)
    def _():
        add(odd_place, odd_target, odd_queue, odd_left, odd_right, odd_total)


def next_kernel(
    even_target, even_place, even_queue, odd_target, odd_place, odd_queue, next_ref,
    even_given, odd_given, even_left, even_right, odd_left, odd_right,
    parts_ref, even_total, odd_total,
):
    groups, sectors, part_rows, size = parts_ref.shape
    odd = lax.rem(lax.axis_index("blk"), 2)

    def finish(place_ref, target_ref, queue, left_ref, right_ref, total):
        def block_of(t):
            return next_ref[pl.ds(pl.multiple_of(place_ref[t] * size, size), size), :]

        add_terms(queue, block_of, target_ref, left_ref, right_ref, total, 7, 3)
        for g in range(groups):
            for s in range(sectors):
                parts_ref[g, s] = total[s, g * part_rows : (g + 1) * part_rows, :].astype(
                    parts_ref.dtype
                )

    @pl.when(odd == 0)
    def _():
        finish(even_place, even_target, even_queue, even_left, even_right, even_total)

    @pl.when(odd == 1)
    def _():
        finish(odd_place, odd_target, odd_queue, odd_left, odd_right, odd_total)


def body(psi, sector_class, left_env, right_env, term_source, term_target):
    sectors, size, _ = psi.shape
    slots = left_env.shape[0]
    owners = lax.axis_size("blk")
    groups = lax.axis_size("mpo")
    part_rows = size // groups
    same_chip = [(i, i ^ 1) for i in range(owners)]
    next_chip = [(i, i - 1 if i % 2 == 0 else i + 1) for i in range(1, owners - 1)]
    params = pltpu.CompilerParams(vmem_limit_bytes=24 * 2**20)
    sums = pltpu.VMEM((sectors + 1, size, size), jnp.float32)
    numbers = pltpu.SMEM((slots,), jnp.int32)
    queue = pltpu.SMEM((slots + 1,), jnp.int32)
    sector_blocks = pltpu.VMEM(psi.shape, psi.dtype)
    sent_rows = pltpu.VMEM((sectors * size + TILE_ROWS, size), psi.dtype)
    loaded = (
        sums,
        pltpu.VMEM(left_env.shape, left_env.dtype),
        pltpu.VMEM(right_env.shape, right_env.dtype),
        numbers, numbers, queue, queue,
    )
    loaded_specs = (VMEM,) * 3 + (SMEM,) * 4
    load_scratch = [numbers, queue]
    load_sems = [DMA((2,)), DMA((2,))]
    tables = tuple(in_hbm(x) for x in (term_source, term_target, left_env, right_env))

    def cost(share):
        return pl.CostEstimate(
            flops=int(4 * slots * size**3 * share),
            bytes_accessed=int(4 * slots * size**2 * share),
            transcendentals=0,
        )

    masked, classes = pl.pallas_call(
        mask_kernel,
        out_shape=(sent_rows, pltpu.SMEM((sectors,), jnp.int32)),
        in_specs=[ANY] * 2,
        out_specs=(VMEM, SMEM),
        scratch_shapes=[sector_blocks, DMA, DMA],
        compiler_params=params,
        name="masked",
    )(in_hbm(sector_class), in_hbm(psi))
    masked, *even = pl.pallas_call(
        early_kernel,
        out_shape=(sent_rows, *loaded),
        in_specs=[ANY] * 4 + [VMEM],
        out_specs=(VMEM, *loaded_specs),
        input_output_aliases={4: 0},
        scratch_shapes=[*load_scratch, *load_sems],
        compiler_params=params,
        name="early_terms",
    )(*tables, in_vmem(masked))
    following = lax.ppermute(masked, "blk", next_chip)
    copied, keep, *odd = pl.pallas_call(
        late_kernel,
        out_shape=(sector_blocks, pltpu.VMEM((sectors, part_rows, size), jnp.float32), *loaded),
        in_specs=[ANY] * 4 + [VMEM, SMEM],
        out_specs=(VMEM, VMEM, *loaded_specs),
        scratch_shapes=[*load_scratch, *load_sems],
        compiler_params=params,
        cost_estimate=cost(1),
        name="late_terms",
    )(*tables, in_vmem(masked), in_smem(classes))
    pair = lax.ppermute(copied, "blk", same_chip)
    even_total, even_left, even_right, even_target, even_place, even_pair, even_next = even
    odd_total, odd_left, odd_right, odd_target, odd_place, odd_pair, odd_next = odd
    envs = tuple(in_vmem(x) for x in (even_left, even_right, odd_left, odd_right))
    even_total, odd_total = pl.pallas_call(
        pair_kernel,
        out_shape=(sums, sums),
        in_specs=[SMEM] * 6 + [VMEM] * 7,
        out_specs=(VMEM,) * 2,
        input_output_aliases={7: 0, 8: 1},
        compiler_params=params,
        cost_estimate=cost(0.001),
        name="pair_terms",
    )(
        *(in_smem(x) for x in (even_target, even_place, even_pair)),
        *(in_smem(x) for x in (odd_target, odd_place, odd_pair)),
        *(in_vmem(x) for x in (pair, even_total, odd_total)),
        *envs,
    )
    parts, _, _ = pl.pallas_call(
        next_kernel,
        out_shape=(pltpu.VMEM((groups, sectors, part_rows, size), jnp.bfloat16), sums, sums),
        in_specs=[SMEM] * 6 + [VMEM] * 7,
        out_specs=(VMEM,) * 3,
        input_output_aliases={7: 1, 8: 2},
        compiler_params=params,
        cost_estimate=cost(0.5),
        name="next_terms",
    )(
        *(in_smem(x) for x in (even_target, even_place, even_next)),
        *(in_smem(x) for x in (odd_target, odd_place, odd_next)),
        *(in_vmem(x) for x in (following, even_total, odd_total)),
        *envs,
    )
    received = lax.all_to_all(parts, "mpo", 0, 0)
    summed = received[0].astype(jnp.float32)
    for g in range(1, groups):
        summed += received[g].astype(jnp.float32)
    return jnp.where(keep != 0, summed, 0.0)


def solution(mesh):
    placed = (
        P("blk", None, None),
        P("blk"),
        P(("blk", "mpo"), None, None),
        P(("blk", "mpo"), None, None),
        P(("blk", "mpo")),
        P(("blk", "mpo")),
    )
    return jax.shard_map(
        body, mesh=mesh, in_specs=placed, out_specs=P("blk", "mpo", None), check_vma=False
    )
```
